256 devices in a mesh: seq: 64 (over z, y_hi, x), head: 4 (over y_lo, core).
Axes of the slice: x: 4, y: 4 (y_hi: 2, y_lo: 2; y = y_hi * 2 + y_lo), z: 8, core: 2. Of those that a mesh axis runs over, the one named last changes fastest.
Arguments:
- queries: bfloat16 [16384, 4096], P('seq', 'head')
- key_states: bfloat16 [16384, 1024], P('seq', 'head')
- value_states: bfloat16 [16384, 1024], P('seq', 'head'), may hold values from -6 to 6
- query_tangent: bfloat16 [16384, 4096], P('seq', 'head'), may hold values from -6 to 6
- key_tangent: bfloat16 [16384, 1024], P('seq', 'head'), may hold values from -6 to 6
- value_tangent: bfloat16 [16384, 1024], P('seq', 'head'), may hold values from -6 to 6
- segment_ids: int32 [16384], P('seq'), may hold values from 0 to 31, never falling along the last dimension, each value on 1 to 1024 neighbouring positions
- out_weight: bfloat16 [4096, 4096], P('head'), may hold values from -0.5 to 0.5
Outputs:
- layer_out: bfloat16 [16384, 4096], P('seq', 'head')
- layer_tangent: bfloat16 [16384, 4096], P('seq', 'head')
The draws below stay inside these ranges and needn't reach their ends.
All inputs are finite; a program needn't handle non-finite values.
Results may differ from the reference program's by a relative error of at most 0.015.
The reference program's roundings to bfloat16 on the way count: a program that leaves them out, or rounds other values in their place, can miss the bound.
Values may be sent and summed in bfloat16 or wider, within the bound.
A program may use at most 128 MiB of HBM per device.

```python
import math
import jax
import jax.numpy as jnp
import numpy as np
from jax import lax

D = 4096
HEADS = 32
KV_HEADS = 8
HD = 128
TOK_DEV = 256
TOKENS = 16384
WINDOW = 768
N_SEQ = 64
N_HEAD = 4


def shared_keys(key):
    return jax.random.normal(jax.random.fold_in(key, 101), (TOKENS, KV_HEADS * HD), jnp.float32)


def draw_key_states(key, part):
    base = shared_keys(key)
    return base.astype(jnp.bfloat16)


def draw_queries(key, part):
    key = jax.random.fold_in(key, 2)
    fresh = jax.random.normal(key, (TOKENS, HEADS * HD), jnp.float32)
    return fresh.astype(jnp.bfloat16)


def spiked(entries, rng, source, target, parts, factor):
    def block_of(dim):
        return (jnp.arange(entries.shape[dim]) // (entries.shape[dim] // parts)).reshape((-1,) + (1,) * (entries.ndim - 1 - dim))

    one_side = jax.random.permutation(rng, parts)[block_of(target)]
    second = (block_of(target) + parts // 2) % parts
    return jnp.where((block_of(source) == one_side) | (block_of(source) == second), factor * entries, entries)


def level_of(own_key, extent, cuts, low, largest):
    def one(axis_at, parts):
        steps = jax.random.uniform(jax.random.fold_in(jax.random.fold_in(own_key, 6), axis_at), (parts,), jnp.float32, low / len(cuts), largest / len(cuts))
        return jnp.repeat(jnp.exp(steps), extent[axis_at] // parts).reshape((-1,) + (1,) * (len(extent) - axis_at - 1))

    gain = one(*cuts[0])
    for cut in cuts[1:]:
        gain = gain * one(*cut)
    return gain


def profile(amount, total, reach, slope):
    weights = [(1 << 20) // math.isqrt(grade ** slope) + 1 for grade in range(2, amount + 1)]
    rest, holding = total - reach - (amount - 1), [1] * (amount - 1)
    while rest > 0:
        movable = [i for i in range(amount - 1) if holding[i] < reach]
        whole, budget = sum([weights[i] for i in movable]), rest
        for i in movable:
            more = min(reach - holding[i], max(1, budget * weights[i] // whole), rest)
            holding[i] = holding[i] + more
            rest = rest - more
    return np.array([reach] + holding)


def ragged_sizes(stream_key, number_of, total, reach, skew):
    if number_of == 2:
        one = jax.random.randint(stream_key, (), max(1, total - reach), min(reach, total - 1) + 1)
        return jnp.stack([one, total - one])
    tallies = jnp.asarray(profile(number_of, total, reach, skew), jnp.int32)
    pairs = (number_of - 1) // 2
    giver, receiver = tallies[1:1 + 2 * pairs:2], tallies[2:2 + 2 * pairs:2]
    slack = jnp.minimum(giver - 1, reach - receiver)
    moved = jax.random.randint(jax.random.fold_in(stream_key, 1), (pairs,), 0, 1 << 20) % (slack + 1)
    tallies = tallies.at[1:1 + 2 * pairs:2].set(giver - moved).at[2:2 + 2 * pairs:2].set(receiver + moved)
    return tallies[jax.random.permutation(jax.random.fold_in(stream_key, 2), number_of)]


def gaussian(rng, dims, deviation, most, cuts=(), held_as=jnp.bfloat16):
    level = level_of(rng, dims, cuts, -0.22, 0.18) if cuts else 1.0
    result = jax.random.normal(rng, dims, jnp.float32) * deviation * level
    return jnp.minimum(jnp.maximum(result, -most), most).astype(held_as)


def bell_draw_with(own_key, dims, spread, most, split, heavy, kind=jnp.bfloat16):
    result = spread * jax.random.normal(own_key, dims, jnp.float32)
    if split:
        result = result * level_of(own_key, dims, split, -0.22, 0.18)
    return jnp.clip(spiked(result, jax.random.fold_in(own_key, 3), *heavy), -most, most).astype(kind)


def setup_inputs(seed: int = 0) -> dict:
    streams_of = jax.random.split(jax.random.key(seed), 9)
    queries = draw_queries(jax.random.fold_in(streams_of[8], 71), 0)
    key_states = draw_key_states(jax.random.fold_in(streams_of[8], 71), 0)
    value_states = gaussian(streams_of[2], (TOKENS, KV_HEADS * HD), 1.0, 6.0, ((0, 64), (1, 4)))
    query_tangent = gaussian(streams_of[3], (TOKENS, HEADS * HD), 1.0, 6.0, ((0, 64), (1, 4)))
    key_tangent = gaussian(streams_of[4], (TOKENS, KV_HEADS * HD), 1.0, 6.0, ((0, 64), (1, 4)))
    value_tangent = gaussian(streams_of[5], (TOKENS, KV_HEADS * HD), 1.0, 6.0, ((0, 64), (1, 4)))
    segment_ids = jnp.searchsorted(jnp.cumsum(ragged_sizes(streams_of[6], N_SEQ // 2, TOKENS, 4 * TOK_DEV, 0)), jnp.arange(TOKENS), side="right").astype(jnp.int32)
    out_weight = bell_draw_with(streams_of[7], (HEADS * HD, D), (HEADS * HD // 16) ** -0.5, 0.5, ((0, 4),), (0, 1, 4, 2.0))
    return dict(queries=queries, key_states=key_states, value_states=value_states, query_tangent=query_tangent, key_tangent=key_tangent, value_tangent=value_tangent, segment_ids=segment_ids, out_weight=out_weight)


negative_fill = -1e+30

def reference(queries, key_states, value_states, query_tangent, key_tangent, value_tangent, segment_ids, out_weight):
    inverse_root = 1.0 / math.sqrt(HD)
    group_size = HEADS // KV_HEADS
    block_count = TOKENS // TOK_DEV
    margin = 3 * TOK_DEV
    span = 4 * TOK_DEV
    filler = jnp.zeros((margin, KV_HEADS * HD), jnp.float32)

    def padded(array):
        return jnp.concatenate([filler, array.astype(jnp.float32)], axis=0)
    key_pad = padded(key_states)
    ktan_pad = padded(key_tangent)
    val_pad = padded(value_states)
    vtan_pad = padded(value_tangent)
    seg_pad = jnp.concatenate([jnp.full((margin,), -1, jnp.int32), segment_ids.astype(jnp.int32)])
    query_blocks = queries.astype(jnp.float32).reshape(block_count, TOK_DEV, KV_HEADS, group_size, HD)
    qtan_blocks = query_tangent.astype(jnp.float32).reshape(block_count, TOK_DEV, KV_HEADS, group_size, HD)
    seg_blocks = segment_ids.reshape(block_count, TOK_DEV)
    block_ids = jnp.arange(block_count, dtype=jnp.int32)

    def one_block(inputs):
        q_heads, qtan_heads, query_seg, block = inputs
        start = (block * TOK_DEV).astype(jnp.int32)

        def window(array):
            return lax.dynamic_slice_in_dim(array, start, span, 0).reshape(span, KV_HEADS, HD)
        key_heads = window(key_pad)
        ktan_heads = window(ktan_pad)
        val_heads = window(val_pad)
        vtan_heads = window(vtan_pad)
        key_seg = lax.dynamic_slice_in_dim(seg_pad, start, span, 0)
        key_pos = start - margin + jnp.arange(span, dtype=jnp.int32)
        query_pos = start + jnp.arange(TOK_DEV, dtype=jnp.int32)
        diff = query_pos[:, None] - key_pos[None, :]
        allowed = (diff >= 0) & (diff < WINDOW) & (key_pos[None, :] >= 0) & (key_seg[None, :] == query_seg[:, None])
        allowed = allowed[:, None, None, :]
        scores = jnp.einsum('qhgd,khd->qhgk', q_heads, key_heads) * inverse_root
        tangent = (jnp.einsum('qhgd,khd->qhgk', qtan_heads, key_heads) + jnp.einsum('qhgd,khd->qhgk', q_heads, ktan_heads)) * inverse_root
        masked = jnp.where(allowed, scores, negative_fill)
        row_max = lax.optimization_barrier(jnp.max(masked, axis=-1))
        weights = jnp.where(allowed, jnp.exp(masked - row_max[..., None]), 0.0)
        weight_sum = lax.optimization_barrier(jnp.sum(weights, axis=-1))
        product = weights * tangent
        tangent_sum = lax.optimization_barrier(jnp.sum(product, axis=-1))
        rounded = lax.optimization_barrier(weights.astype(jnp.bfloat16)).astype(jnp.float32)
        weighted = lax.optimization_barrier(product.astype(jnp.bfloat16)).astype(jnp.float32)
        accum = jnp.einsum('qhgk,khd->qhgd', rounded, val_heads)
        accum_tan = jnp.einsum('qhgk,khd->qhgd', rounded, vtan_heads) + jnp.einsum('qhgk,khd->qhgd', weighted, val_heads)
        mixed = accum / weight_sum[..., None]
        mixed_tan = accum_tan / weight_sum[..., None] - (tangent_sum / weight_sum)[..., None] * mixed
        return (mixed.astype(jnp.bfloat16).reshape(TOK_DEV, HEADS * HD), mixed_tan.astype(jnp.bfloat16).reshape(TOK_DEV, HEADS * HD))
    attended, attended_tan = lax.map(one_block, (query_blocks, qtan_blocks, seg_blocks, block_ids))
    attended = attended.reshape(TOKENS, HEADS * HD)
    attended_tan = attended_tan.reshape(TOKENS, HEADS * HD)
    group_rows = HEADS * HD // N_HEAD
    out_total = jnp.zeros((TOKENS, D), jnp.float32)
    tan_total = jnp.zeros((TOKENS, D), jnp.float32)
    for group in range(N_HEAD):
        rows = out_weight[group * group_rows:(group + 1) * group_rows]
        out_part = jnp.dot(attended[:, group * group_rows:(group + 1) * group_rows], rows, preferred_element_type=jnp.float32)
        tan_part = jnp.dot(attended_tan[:, group * group_rows:(group + 1) * group_rows], rows, preferred_element_type=jnp.float32)
        out_total = out_total + lax.optimization_barrier(out_part.astype(jnp.bfloat16)).astype(jnp.float32)
        tan_total = tan_total + lax.optimization_barrier(tan_part.astype(jnp.bfloat16)).astype(jnp.float32)
    return (out_total.astype(jnp.bfloat16), tan_total.astype(jnp.bfloat16))
```

```python
import functools
import math

import jax
import jax.numpy as jnp
from jax import lax
from jax.experimental import pallas as pl
from jax.experimental.pallas import tpu as pltpu
from jax.sharding import PartitionSpec as P

HD = 128
ROWS = 256
LANES = 128
TILE = 64
TILES = ROWS // TILE
GROUP = 4
KV_LOCAL = 2
RING = 4
WIDE = 1024
PIECE = 512
PIECES = WIDE // PIECE
CHUNKS = 8
PART = ROWS // CHUNKS
CHUNK_ROWS = 4 * PART + 16
SLOTS = 6
HANDS = 2
FILL = -3e38
SCALE = 1.0 / math.sqrt(HD)
LOG2E = math.log2(math.e)
MESH = pl.DeviceIdType.MESH
F32 = jnp.float32
BF16 = jnp.bfloat16


SEND, WAIT = 0, 1
ALL, INNER, OUTER = 0, 1, 2
SCRIPT = (
    (
        (
            (SEND, 0, 1, 0, 1, ALL),
            (SEND, 0, 3, 0, 3, ALL),
            (SEND, 0, 1, 1, 1, ALL),
            (SEND, 0, 3, 1, 3, ALL),
            (SEND, 0, 1, 2, 1, ALL),
            (SEND, 0, 3, 2, 3, ALL),
            (SEND, 0, 1, 3, 1, ALL),
            (SEND, 0, 3, 3, 3, ALL),
            (SEND, 0, 1, 4, 1, ALL),
            (SEND, 0, 1, 5, 1, ALL),
            (SEND, 0, 1, 6, 1, ALL),
            (SEND, 0, 1, 7, 1, ALL),
        ),
        (
            (WAIT, 4, 0, ALL),
            (SEND, 4, 2, 0, 3, ALL),
            (SEND, 4, 3, 0, 4, OUTER),
            (WAIT, 5, 5, OUTER),
            (SEND, 5, 2, 5, 4, OUTER),
            (WAIT, 4, 1, ALL),
            (SEND, 4, 2, 1, 3, ALL),
            (SEND, 4, 3, 1, 4, OUTER),
            (WAIT, 5, 6, OUTER),
            (SEND, 5, 2, 6, 4, OUTER),
            (WAIT, 4, 2, ALL),
            (SEND, 4, 2, 2, 3, ALL),
            (SEND, 4, 3, 2, 4, OUTER),
            (WAIT, 5, 7, OUTER),
            (SEND, 5, 2, 7, 4, OUTER),
            (WAIT, 4, 3, ALL),
            (SEND, 4, 2, 3, 3, ALL),
            (SEND, 4, 3, 3, 4, OUTER),
            (WAIT, 1, 0, INNER),
            (SEND, 1, 2, 0, 1, INNER),
            (WAIT, 4, 4, ALL),
            (SEND, 4, 2, 4, 3, ALL),
            (SEND, 4, 3, 4, 4, OUTER),
            (WAIT, 1, 1, INNER),
            (SEND, 1, 2, 1, 1, INNER),
            (WAIT, 4, 5, ALL),
            (SEND, 4, 2, 5, 3, ALL),
            (SEND, 4, 3, 5, 4, OUTER),
            (SEND, 0, 3, 4, 3, ALL),
            (SEND, 0, 3, 5, 3, ALL),
            (SEND, 0, 3, 6, 3, ALL),
            (SEND, 0, 3, 7, 3, ALL),
            (WAIT, 1, 2, INNER),
            (SEND, 1, 2, 2, 1, INNER),
            (WAIT, 4, 6, OUTER),
            (SEND, 4, 3, 6, 4, OUTER),
            (WAIT, 1, 3, INNER),
            (SEND, 1, 2, 3, 1, INNER),
            (WAIT, 4, 7, OUTER),
            (SEND, 4, 3, 7, 4, OUTER),
            (WAIT, 1, 4, INNER),
            (SEND, 1, 2, 4, 1, INNER),
        ),
        (
        ),
    ),
    (
        (
            (SEND, 0, 1, 0, 2, ALL),
            (SEND, 0, 4, 0, 0, ALL),
            (SEND, 0, 1, 1, 2, ALL),
            (SEND, 0, 4, 1, 0, ALL),
            (SEND, 0, 1, 2, 2, ALL),
            (SEND, 0, 4, 2, 0, ALL),
            (SEND, 0, 1, 3, 2, ALL),
            (SEND, 0, 4, 3, 0, ALL),
            (SEND, 0, 1, 4, 2, ALL),
            (SEND, 0, 4, 4, 0, ALL),
            (SEND, 0, 1, 5, 2, ALL),
            (SEND, 0, 4, 5, 0, ALL),
            (SEND, 0, 1, 6, 2, ALL),
            (SEND, 0, 4, 6, 0, OUTER),
            (SEND, 0, 1, 7, 2, ALL),
            (SEND, 0, 4, 7, 0, OUTER),
        ),
        (
            (WAIT, 4, 5, OUTER),
            (SEND, 4, 2, 5, 4, OUTER),
            (WAIT, 4, 6, OUTER),
            (SEND, 4, 2, 6, 4, OUTER),
            (WAIT, 4, 7, OUTER),
            (SEND, 4, 2, 7, 4, OUTER),
            (WAIT, 3, 0, INNER),
            (SEND, 3, 2, 0, 0, INNER),
            (WAIT, 1, 4, ALL),
            (SEND, 1, 2, 4, 2, ALL),
            (WAIT, 3, 1, INNER),
            (SEND, 3, 2, 1, 0, INNER),
            (WAIT, 1, 5, ALL),
            (SEND, 1, 2, 5, 2, ALL),
            (WAIT, 3, 2, INNER),
            (SEND, 3, 2, 2, 0, INNER),
            (WAIT, 1, 6, ALL),
            (SEND, 1, 2, 6, 2, ALL),
            (WAIT, 3, 3, INNER),
            (SEND, 3, 2, 3, 0, INNER),
            (WAIT, 1, 7, ALL),
            (SEND, 1, 2, 7, 2, ALL),
            (WAIT, 3, 4, INNER),
            (SEND, 3, 2, 4, 0, INNER),
        ),
        (
        ),
    ),
    (
        (
            (SEND, 0, 5, 5, 0, OUTER),
            (SEND, 0, 5, 6, 0, OUTER),
            (SEND, 0, 5, 7, 0, OUTER),
            (SEND, 0, 4, 0, 4, OUTER),
            (SEND, 0, 1, 0, 3, ALL),
            (SEND, 0, 4, 1, 4, OUTER),
            (SEND, 0, 1, 1, 3, ALL),
            (SEND, 0, 4, 2, 4, OUTER),
            (SEND, 0, 1, 2, 3, ALL),
            (SEND, 0, 4, 3, 4, OUTER),
            (SEND, 0, 1, 3, 3, ALL),
            (SEND, 0, 4, 4, 4, OUTER),
            (SEND, 0, 1, 4, 3, ALL),
            (SEND, 0, 4, 5, 4, OUTER),
            (SEND, 0, 1, 5, 3, ALL),
            (SEND, 0, 4, 6, 4, OUTER),
            (SEND, 0, 1, 6, 3, ALL),
            (SEND, 0, 4, 7, 4, OUTER),
            (SEND, 0, 1, 7, 3, ALL),
        ),
        (
            (WAIT, 4, 0, INNER),
            (SEND, 4, 3, 0, 1, INNER),
            (WAIT, 4, 1, INNER),
            (SEND, 4, 3, 1, 1, INNER),
            (WAIT, 4, 2, INNER),
            (SEND, 4, 3, 2, 1, INNER),
            (WAIT, 4, 3, INNER),
            (SEND, 4, 3, 3, 1, INNER),
            (WAIT, 4, 4, INNER),
            (SEND, 4, 3, 4, 1, INNER),
            (WAIT, 4, 5, INNER),
            (SEND, 4, 3, 5, 1, INNER),
            (WAIT, 1, 6, ALL),
            (SEND, 1, 2, 6, 3, ALL),
            (WAIT, 4, 6, INNER),
            (SEND, 4, 3, 6, 1, INNER),
            (WAIT, 1, 7, ALL),
            (SEND, 1, 2, 7, 3, ALL),
            (WAIT, 4, 7, INNER),
            (SEND, 4, 3, 7, 1, INNER),
        ),
        (
        ),
    ),
    (
        (
            (SEND, 0, 4, 5, 1, OUTER),
            (SEND, 0, 4, 6, 1, OUTER),
            (SEND, 0, 4, 7, 1, OUTER),
            (SEND, 0, 4, 0, 4, OUTER),
            (SEND, 0, 4, 1, 4, OUTER),
            (SEND, 0, 4, 2, 4, OUTER),
            (SEND, 0, 4, 3, 4, OUTER),
            (SEND, 0, 4, 4, 4, OUTER),
            (SEND, 0, 4, 5, 4, OUTER),
            (SEND, 0, 4, 6, 4, OUTER),
            (SEND, 0, 4, 7, 4, OUTER),
        ),
        (
            (WAIT, 3, 0, ALL),
            (SEND, 3, 2, 0, 2, ALL),
            (WAIT, 4, 0, INNER),
            (SEND, 4, 1, 0, 0, INNER),
            (SEND, 4, 3, 0, 2, INNER),
            (WAIT, 3, 1, ALL),
            (SEND, 3, 2, 1, 2, ALL),
            (WAIT, 4, 1, INNER),
            (SEND, 4, 1, 1, 0, INNER),
            (SEND, 4, 3, 1, 2, INNER),
            (WAIT, 3, 2, ALL),
            (SEND, 3, 2, 2, 2, ALL),
            (WAIT, 4, 2, INNER),
            (SEND, 4, 1, 2, 0, INNER),
            (SEND, 4, 3, 2, 2, INNER),
            (WAIT, 3, 3, ALL),
            (SEND, 3, 2, 3, 2, ALL),
            (WAIT, 4, 3, INNER),
            (SEND, 4, 1, 3, 0, INNER),
            (SEND, 4, 3, 3, 2, INNER),
            (WAIT, 4, 4, INNER),
            (SEND, 4, 1, 4, 0, INNER),
            (SEND, 4, 3, 4, 2, INNER),
            (WAIT, 4, 5, INNER),
            (SEND, 4, 1, 5, 0, INNER),
            (SEND, 4, 3, 5, 2, INNER),
            (WAIT, 4, 6, INNER),
            (SEND, 4, 1, 6, 0, INNER),
            (SEND, 4, 3, 6, 2, INNER),
            (WAIT, 4, 7, INNER),
            (SEND, 4, 1, 7, 0, INNER),
            (SEND, 4, 3, 7, 2, INNER),
        ),
        (
        ),
    ),
)
MOST = max(sum(op[0] == SEND for phase in script for op in phase) for script in SCRIPT)


def dot(a, b):
    return lax.dot_general(a, b, (((1,), (0,)), ((), ())), preferred_element_type=F32)


def dot_t(a, b):
    return lax.dot_general(a, b, (((1,), (1,)), ((), ())), preferred_element_type=F32)


def both(a):
    return jnp.concatenate([a, a], axis=-1)


def kernel(
    n_seq,
    q_hbm, k_hbm, v_hbm, qt_hbm, kt_hbm, vt_hbm, seg_ref, w_hbm,
    out_hbm, tan_hbm,
    qbuf, qtbuf, kv, wbuf, att, rs_out, rs_in, own, acc, tsum, mref, lref, out_ref, tan_ref,
    load_sem, q_sem, w_sem, wx_send, wx_recv, halo_send, halo_recv,
    att_send, att_recv, rs_send, rs_recv, store_sem,
):
    seq = lax.axis_index("seq")
    head = lax.axis_index("head")
    x = lax.rem(seq, RING)
    base = seq - x
    not_first = seq >= RING
    not_last = seq < n_seq - RING
    core = lax.rem(head, 2)
    y_lo = head // 2
    other_core = {"seq": seq, "head": y_lo * 2 + 1 - core}
    other_chip = {"seq": seq, "head": (1 - y_lo) * 2 + core}
    peers = [{"seq": base + lax.rem(x + d, RING), "head": head} for d in (1, 2, 3)]
    after = {"seq": lax.rem(seq + RING, n_seq), "head": head}
    before = {"seq": lax.rem(seq + n_seq - RING, n_seq), "head": head}

    barrier = pltpu.get_barrier_semaphore()
    for target in (*peers, before, other_core, other_chip):
        pl.semaphore_signal(barrier, inc=1, device_id=target, device_id_type=MESH)

    kv_loads = []
    for a, ref in enumerate((k_hbm, kt_hbm, v_hbm, vt_hbm)):
        kv_loads.append(
            pltpu.make_async_copy(ref, kv.at[0, :, pl.ds(a * PART, PART)], load_sem.at[a])
        )
    q_loads = [
        pltpu.make_async_copy(q_hbm, qbuf, q_sem.at[0]),
        pltpu.make_async_copy(qt_hbm, qtbuf, q_sem.at[1]),
    ]
    w_loads = []
    for yb in range(2):
        w_loads.append(
            pltpu.make_async_copy(
                w_hbm.at[:, pl.ds(pl.multiple_of((yb * 2 + core) * WIDE, WIDE), WIDE)],
                wbuf.at[core, yb],
                w_sem.at[yb],
            )
        )
    for load in kv_loads + q_loads:
        load.start()

    seg_row = seg_ref[...].astype(F32)
    kv[0, CHUNKS - 1, 4 * PART :, :] = jnp.broadcast_to(seg_row, (16, ROWS)).astype(BF16)
    for load in kv_loads:
        load.wait()
    pl.semaphore_wait(barrier, 6)

    def remote(src, dst, send, recv, target):
        return pltpu.make_async_remote_copy(
            src_ref=src, dst_ref=dst, send_sem=send, recv_sem=recv,
            device_id=target, device_id_type=MESH,
        )

    def flagged(flag, act):
        if flag:
            pl.when(not_first if flag == INNER else not_last)(act)
        else:
            act()

    def halo(src, dst, c, index, target):
        place = after if target == RING else {"seq": base + target, "head": head}
        rows = pl.ds(0, CHUNK_ROWS if c == 0 else 4 * PART)
        return remote(
            kv.at[src, CHUNKS - 1 - c, rows], kv.at[dst, CHUNKS - 1 - c, rows],
            halo_send.at[index], halo_recv.at[dst - 1, c], place,
        )

    def got(slot, c):
        halo(0, slot, c, 0, RING).wait_recv()

    def run(phase):
        for at in range(RING):
            @pl.when(x == at)
            def _():
                index = sum(op[0] == SEND for done in SCRIPT[at][:phase] for op in done)
                for op in SCRIPT[at][phase]:
                    if op[0] == SEND:
                        _, src, dst, c, target, flag = op
                        flagged(flag, halo(src, dst, c, index, target).start)
                        index += 1
                    else:
                        _, slot, c, flag = op
                        flagged(flag, functools.partial(got, slot, c))

    run(0)

    w_swaps = []
    for yb in range(2):
        w_swaps.append(
            remote(
                w_hbm.at[:, pl.ds(pl.multiple_of((yb * 2 + 1 - core) * WIDE, WIDE), WIDE)],
                wbuf.at[core, yb],
                wx_send.at[yb],
                wx_recv.at[yb],
                other_core,
            )
        )
    for copy in w_swaps + w_loads:
        copy.start()

    def arrive(slot, chunks):
        for at in range(RING):
            seen = {op[1:3] for phase in SCRIPT[at] for op in phase if op[0] == WAIT}
            left = [c for c in chunks if (slot, c) not in seen]
            if left:
                @pl.when((x == at) & (seq >= slot))
                def _():
                    for c in left:
                        got(slot, c)

    row_id = lax.broadcasted_iota(jnp.int32, (TILE, ROWS), 0)
    col_id = lax.broadcasted_iota(jnp.int32, (TILE, ROWS), 1)

    def seg_column(tile):
        spread = jnp.where(row_id + tile * TILE == col_id, jnp.broadcast_to(seg_row, (TILE, ROWS)), 0.0)
        return jnp.sum(spread, axis=1, keepdims=True)

    seg_q = [seg_column(tile) for tile in range(TILES)]

    def fold(tile, slot, chunks, first=False):
        if not first:
            @pl.when(seq >= slot)
            def _():
                fold_in(tile, slot, chunks, False)
        else:
            fold_in(tile, slot, chunks, True)

    def fold_in(tile, slot, chunks, first):
        width = PART * len(chunks)
        begin = (CHUNKS - 1 - chunks[0]) * PART
        rows = slice(tile * TILE, (tile + 1) * TILE)
        seg_k = kv[slot, CHUNKS - 1, 4 * PART : 4 * PART + 16, :].astype(F32)[0:1, begin : begin + width]
        ok = jnp.broadcast_to(seg_q[tile], (TILE, width)) == jnp.broadcast_to(seg_k, (TILE, width))
        if slot in (0, 3):
            row_at = lax.broadcasted_iota(jnp.int32, (TILE, width), 0) + tile * TILE
            col_at = lax.broadcasted_iota(jnp.int32, (TILE, width), 1) + begin
            ok = ok & ((col_at <= row_at) if slot == 0 else (col_at > row_at))
        bias = jnp.where(ok, 0.0, FILL)

        def block(a, g):
            return jnp.concatenate(
                [
                    kv[slot, CHUNKS - 1 - c, a * PART : (a + 1) * PART, g * HD : (g + 1) * HD]
                    for c in chunks
                ],
                axis=0,
            )

        for g in range(KV_LOCAL):
            heads = [slice((g * GROUP + j) * HD, (g * GROUP + j + 1) * HD) for j in range(GROUP)]
            qs = jnp.concatenate([qbuf[rows, h] for h in heads], axis=0)
            qts = jnp.concatenate([qtbuf[rows, h] for h in heads], axis=0)
            k, kt, v, vt = (block(a, g) for a in range(4))
            s = dot_t(qs, k)
            t = dot_t(jnp.concatenate([qts, qs], axis=1), jnp.concatenate([k, kt], axis=1))
            s = (s * (SCALE * LOG2E)).reshape(GROUP, TILE, width) + bias[None]
            s = s.reshape(GROUP * TILE, width)
            top = jnp.max(s, axis=1, keepdims=True)
            if first:
                m_new = jnp.broadcast_to(top, (GROUP * TILE, HD))
            else:
                m_old = mref[tile, g]
                m_new = jnp.maximum(m_old, top)
                alpha = jnp.exp2(m_old - m_new)
            mref[tile, g] = m_new
            p = jnp.exp2(s - (both(m_new) if width == 2 * LANES else m_new))
            l = p[:, :LANES] + p[:, LANES:] if width == 2 * LANES else p
            wt = (p * (t * SCALE)).astype(BF16)
            pb = p.astype(BF16)
            o = dot(pb, jnp.concatenate([v, vt], axis=1))
            o2 = dot(wt, jnp.concatenate([v, jnp.ones((width, HD), BF16)], axis=1))
            tan = o[:, HD:] + o2[:, :HD]
            if first:
                lref[tile, g] = l
                acc[tile, g, :, 0:HD] = o[:, :HD]
                acc[tile, g, :, HD:] = tan
                tsum[tile, g] = o2[:, HD:]
            else:
                lref[tile, g] = lref[tile, g] * alpha + l
                acc[tile, g, :, 0:HD] = acc[tile, g, :, 0:HD] * alpha + o[:, :HD]
                acc[tile, g, :, HD:] = acc[tile, g, :, HD:] * alpha + tan
                tsum[tile, g] = tsum[tile, g] * alpha + o2[:, HD:]

    def finish(tile):
        for g in range(KV_LOCAL):
            finish_one(tile, g)
            att_copy(tile, g).start()

    def finish_one(tile, g):
        total = jnp.sum(lref[tile, g], axis=1, keepdims=True)
        inv = jnp.broadcast_to(1.0 / total, (GROUP * TILE, HD))
        mixed = acc[tile, g, :, 0:HD] * inv
        tangent = acc[tile, g, :, HD:] * inv - (tsum[tile, g] * inv) * mixed
        mixed = mixed.astype(BF16)
        tangent = tangent.astype(BF16)
        for j in range(GROUP):
            lanes = slice(j * HD, (j + 1) * HD)
            att[tile, core, g, 0:TILE, lanes] = mixed[j * TILE : (j + 1) * TILE]
            att[tile, core, g, TILE:, lanes] = tangent[j * TILE : (j + 1) * TILE]

    def att_copy(tile, g):
        return remote(
            att.at[tile, core, g], att.at[tile, core, g],
            att_send.at[tile, g], att_recv.at[tile, g], other_core,
        )

    def swapped(tile):
        for g in range(KV_LOCAL):
            att_copy(tile, g).wait_recv()

    def rs_copy(tile, n):
        return remote(
            rs_out.at[tile, n], rs_in.at[tile, n], rs_send.at[tile, n], rs_recv.at[tile, n], other_chip
        )

    def project(tile, yb, n):
        lanes = slice(n * PIECE, (n + 1) * PIECE)
        total = None
        for c in range(2):
            left = jnp.concatenate([att[tile, c, g] for g in range(KV_LOCAL)], axis=1)
            part = dot(left, wbuf[c, yb, :, lanes])
            total = part if total is None else total + part
        return total

    def send_parts(tile):
        for n in range(PIECES):
            rs_out[tile, n] = project(tile, 1 - y_lo, n).astype(BF16)
            rs_copy(tile, n).start()

    def own_parts(tile):
        for n in range(PIECES):
            own[tile, n] = project(tile, y_lo, n)

    def stores(tile, n):
        part = (pl.ds(tile * TILE, TILE), pl.ds(n * PIECE, PIECE))
        return [
            pltpu.make_async_copy(out_ref.at[part], out_hbm.at[part], store_sem.at[tile, n, 0]),
            pltpu.make_async_copy(tan_ref.at[part], tan_hbm.at[part], store_sem.at[tile, n, 1]),
        ]

    def final(tile):
        rows = slice(tile * TILE, (tile + 1) * TILE)
        for n in range(PIECES):
            rs_copy(tile, n).wait_recv()
            total = (own[tile, n] + rs_in[tile, n].astype(F32)).astype(BF16)
            lanes = slice(n * PIECE, (n + 1) * PIECE)
            out_ref[rows, lanes] = total[:TILE]
            tan_ref[rows, lanes] = total[TILE:]
            for copy in stores(tile, n):
                copy.start()

    every = tuple(range(CHUNKS - 1, -1, -1))
    low, high = every[: CHUNKS // 2], every[CHUNKS // 2 :]
    for load in q_loads:
        load.wait()
    for tile in (3, 2, 1, 0):
        fold(tile, 0, every if tile >= 2 else low, first=True)
    run(1)
    for copy in w_swaps:
        copy.wait_recv()
    for copy in w_loads:
        copy.wait()
    arrive(1, every)
    fold(3, 1, every)
    arrive(3, high)
    fold(3, 3, high)
    arrive(2, every)
    fold(3, 2, every)
    finish(3)
    fold(2, 1, every)
    fold(2, 3, high)
    fold(2, 2, every)
    finish(2)
    swapped(3)
    send_parts(3)
    fold(1, 1, every)
    fold(1, 2, every)
    swapped(2)
    send_parts(2)
    arrive(3, low)
    fold(1, 3, every)
    finish(1)
    fold(0, 1, every)
    fold(0, 2, every)
    swapped(1)
    send_parts(1)
    fold(0, 3, every)
    finish(0)
    own_parts(3)
    own_parts(2)
    swapped(0)
    send_parts(0)
    own_parts(1)
    own_parts(0)
    for tile in (3, 2, 1, 0):
        final(tile)

    for at in range(RING):
        @pl.when(x == at)
        def _():
            index = 0
            for op in (op for phase in SCRIPT[at] for op in phase if op[0] == SEND):
                _, src, dst, c, target, flag = op
                flagged(flag, halo(src, dst, c, index, target).wait_send)
                index += 1
    for copy in w_swaps:
        copy.wait_send()
    for tile in range(TILES):
        for g in range(KV_LOCAL):
            att_copy(tile, g).wait_send()
        for n in range(PIECES):
            rs_copy(tile, n).wait_send()
            for copy in stores(tile, n):
                copy.wait()


def copy_kernel(a_hbm, b_hbm, c_hbm, d_hbm, a_buf, b_buf, load_sem, store_sem):
    loads, stores = [], []
    for i in range(HANDS):
        rows = pl.ds(i * ROWS // HANDS, ROWS // HANDS)
        for j, (src, buf, dst) in enumerate(((a_hbm, a_buf, c_hbm), (b_hbm, b_buf, d_hbm))):
            loads.append(pltpu.make_async_copy(src.at[rows], buf.at[rows], load_sem.at[i, j]))
            stores.append(pltpu.make_async_copy(buf.at[rows], dst.at[rows], store_sem.at[i, j]))
    for load in loads:
        load.start()
    for load, store in zip(loads, stores):
        load.wait()
        store.start()
    for store in stores:
        store.wait()


def solution(mesh):
    n_seq = mesh.shape["seq"]

    def per_device(q, k, v, qt, kt, vt, seg, w):
        dma = pltpu.SemaphoreType.DMA
        anywhere = pl.BlockSpec(memory_space=pl.ANY)
        vmem = pl.BlockSpec(memory_space=pltpu.VMEM)
        stats = (TILES, KV_LOCAL, GROUP * TILE, HD)
        results = [jax.ShapeDtypeStruct((ROWS, WIDE), BF16)] * 2
        outs = pl.pallas_call(
            functools.partial(kernel, n_seq),
            out_shape=results,
            in_specs=[anywhere] * 6 + [vmem, anywhere],
            out_specs=[anywhere, anywhere],
            scratch_shapes=[
                pltpu.VMEM((ROWS, WIDE), BF16),
                pltpu.VMEM((ROWS, WIDE), BF16),
                pltpu.VMEM((SLOTS, CHUNKS, CHUNK_ROWS, 2 * HD), BF16),
                pltpu.VMEM((2, 2, WIDE, WIDE), BF16),
                pltpu.VMEM((TILES, 2, KV_LOCAL, 2 * TILE, WIDE // KV_LOCAL), BF16),
                pltpu.VMEM((TILES, PIECES, 2 * TILE, PIECE), BF16),
                pltpu.VMEM((TILES, PIECES, 2 * TILE, PIECE), BF16),
                pltpu.VMEM((TILES, PIECES, 2 * TILE, PIECE), F32),
                pltpu.VMEM((TILES, KV_LOCAL, GROUP * TILE, 2 * HD), F32),
                pltpu.VMEM(stats, F32),
                pltpu.VMEM(stats, F32),
                pltpu.VMEM(stats, F32),
                pltpu.VMEM((ROWS, WIDE), BF16),
                pltpu.VMEM((ROWS, WIDE), BF16),
                dma((4,)),
                dma((2,)),
                dma((2,)),
                dma((2,)),
                dma((2,)),
                dma((MOST,)),
                dma((SLOTS - 1, CHUNKS)),
                dma((TILES, KV_LOCAL)),
                dma((TILES, KV_LOCAL)),
                dma((TILES, PIECES)),
                dma((TILES, PIECES)),
                dma((TILES, PIECES, 2)),
            ],
            compiler_params=pltpu.CompilerParams(
                collective_id=0, has_side_effects=True, vmem_limit_bytes=56 << 20
            ),
            cost_estimate=pl.CostEstimate(
                flops=8 << 30, bytes_accessed=14 << 20, transcendentals=1 << 21
            ),
            name="tangent_layer",
        )(q, *(a.reshape(CHUNKS, PART, 2 * HD) for a in (k, v)), qt,
          *(a.reshape(CHUNKS, PART, 2 * HD) for a in (kt, vt)), seg.reshape(1, ROWS), w)
        return pl.pallas_call(
            copy_kernel,
            out_shape=results,
            in_specs=[anywhere, anywhere],
            out_specs=[anywhere, anywhere],
            scratch_shapes=[
                pltpu.VMEM((ROWS, WIDE), BF16),
                pltpu.VMEM((ROWS, WIDE), BF16),
                dma((HANDS, 2)),
                dma((HANDS, 2)),
            ],
            cost_estimate=pl.CostEstimate(flops=0, bytes_accessed=2 << 20, transcendentals=0),
            name="hand_over",
        )(*outs)

    return jax.shard_map(
        per_device,
        mesh=mesh,
        in_specs=(
            P("seq", "head"),
            P("seq", "head"),
            P("seq", "head"),
            P("seq", "head"),
            P("seq", "head"),
            P("seq", "head"),
            P("seq"),
            P("head", None),
        ),
        out_specs=(P("seq", "head"), P("seq", "head")),
        check_vma=False,
    )
```
